32 devices in a mesh: runs: 2 (over y), sec: 4 (over z), ops: 2 (over x), sub: 2 (over core).
Axes of the slice: x: 2, y: 2, z: 4, core: 2. Of those that a mesh axis runs over, the one named last changes fastest.
Arguments:
- psi: bfloat16 [4, 4, 4, 128, 512], P('runs', 'sec', None, None, 'sub'), parts along dimension 0, may hold values from -6 to 6
- left_op: bfloat16 [16, 4, 128, 128], P(('runs', 'ops'), 'sec'), parts along dimension 0, may hold values from -0.5 to 0.5
- right_op: bfloat16 [16, 4, 512, 512], P(('runs', 'ops'), 'sec', None, 'sub'), parts along dimension 0, may hold values from -0.09375 to 0.09375
- sector_rows: int32 [8], P('runs'), parts along dimension 0, may hold values from 32 to 128, as said below
- block_live: int32 [8, 4], P('runs'), parts along dimension 0, may hold values 0 or 1
Outputs:
- sigma: bfloat16 [4, 4, 4, 128, 512], P('runs', None, 'sec', 'ops', 'sub'), parts along dimension 0
The draws below stay inside these ranges and needn't reach their ends.
There are 2 independent parts, one for each index of `runs`. The reference program is written for one: setup_inputs(seed, part) draws one part's arguments, and reference() takes and returns one part's arrays. A program takes and returns all parts, laid end to end along the dimension named above; each array names one. Nothing has to cross between parts.
Inputs may be any that keep to these rules, and one draw needn't show every extreme that they name: `sector_rows`: the number of row slots that each left sector uses; some sector uses all 128.
All inputs are finite; a program needn't handle non-finite values.
Results may differ from the reference program's by a relative error of at most 0.0059.
Values may be sent and summed in bfloat16 or wider, within the bound.
No kernel may reach another device: no remote copies, remote signals or barrier semaphores. Data moves between devices by JAX's collectives and lax.ppermute only.
A program may use at most 64 MiB of HBM per device.

```python
import jax
import jax.numpy as jnp
from jax import lax

RB = 128
CB = 512
TERM_DEV = 4
NVEC = 2
NS = 4
NT = 8
N_OPS = 2


def draw_sector_rows(key, part):
    key = jax.random.fold_in(key, 11)
    first_key, second_key = jax.random.split(key)
    counts = jax.random.randint(first_key, (NS,), RB // 4, RB + 1)
    place = jax.random.randint(second_key, (), 0, NS)
    return jnp.where(jnp.arange(NS) == place, RB, counts).astype(jnp.int32)


def plant(entries, own_key, low, high):
    spot = [jax.random.randint(jax.random.fold_in(own_key, axis), (), 0, length) for axis, length in enumerate(entries.shape)]
    widest = entries.shape.index(max(entries.shape))
    beside = spot[:widest] + [(spot[widest] + 1) % entries.shape[widest]] + spot[widest + 1:]
    return entries.at[tuple(spot)].set(low).at[tuple(beside)].set(high)


def levels(key, extent, cuts, least, top_value):
    def one(position, shards_of):
        draws = jax.random.uniform(jax.random.fold_in(jax.random.fold_in(key, 6), position), (shards_of,), jnp.float32, least / len(cuts), top_value / len(cuts))
        return jnp.repeat(jnp.exp(draws), extent[position] // shards_of).reshape((-1,) + (1,) * (len(extent) - position - 1))

    factor_of = one(*cuts[0])
    for cut in cuts[1:]:
        factor_of = factor_of * one(*cut)
    return factor_of


def bell_draw(rng, shape, width, bound, cuts=(), dtype=jnp.bfloat16):
    entries = width * jax.random.normal(rng, shape, jnp.float32)
    if cuts:
        entries = entries * levels(rng, shape, cuts, -0.22, 0.18)
    return jnp.clip(entries, -bound, bound).astype(dtype)


def setup_inputs(seed: int = 0, part: int = 0) -> dict:
    key_list = jax.random.split(jax.random.key(seed), 6)
    part_splits = jax.random.split(jax.random.fold_in(key_list[5], part), 6)
    return {
        "psi": bell_draw(part_splits[0], (NVEC, NS, NS, RB, CB), 1.0, 6.0, ((1, 4), (4, 2))),
        "left_op": bell_draw(part_splits[1], (NT, NS, RB, RB), RB ** -0.5, 0.5, ((0, 2), (1, 4))),
        "right_op": bell_draw(part_splits[2], (NT, NS, CB, CB), (CB * NT) ** -0.5, 0.09375, ((0, 2), (1, 4), (3, 2))),
        "sector_rows": draw_sector_rows(jax.random.fold_in(jax.random.fold_in(key_list[5], part), 71), part),
        "block_live": plant((jax.random.randint(part_splits[4], (NS, NS), 0, 4) < 3).astype(jnp.int32), jax.random.fold_in(part_splits[4], 1), 0, 1),
    }


def reference(psi, left_op, right_op, sector_rows, block_live):
    row_ids = lax.broadcasted_iota(jnp.int32, (NS, RB), 1)
    row_keep = row_ids < sector_rows[:, None]
    keep = row_keep[:, None, :, None] & (block_live[:, :, None, None] > 0)
    masked = jnp.where(keep[None], psi, jnp.zeros_like(psi)).astype(jnp.float32)
    lefts = left_op.reshape(N_OPS, TERM_DEV, NS, RB, RB)
    rights = right_op.reshape(N_OPS, TERM_DEV, NS, CB, CB)

    def one_term(acc, pair):
        left_t, right_t = pair
        left_part = jnp.einsum('aij,vacjk->vacik', left_t.astype(jnp.float32), masked).astype(jnp.bfloat16)
        left_part = lax.optimization_barrier(left_part).astype(jnp.float32)
        return acc + jnp.einsum('vacik,ckl->vacil', left_part, right_t.astype(jnp.float32)), None

    def one_group(total, pair):
        start = jnp.zeros((NVEC, NS, NS, RB, CB), jnp.float32)
        partial_value, unused = lax.scan(one_term, start, pair)
        rounded = lax.optimization_barrier(partial_value.astype(jnp.bfloat16))
        return total + rounded.astype(jnp.float32), None

    total, unused = lax.scan(one_group, jnp.zeros((NVEC, NS, NS, RB, CB), jnp.float32), (lefts, rights))
    total = jnp.where(keep[None], total, jnp.zeros_like(total))
    return total.astype(jnp.bfloat16)
```

```python
import functools
import itertools

import jax
import jax.numpy as jnp
from jax import lax
from jax.experimental import pallas as pl
from jax.experimental.pallas import tpu as pltpu
from jax.sharding import PartitionSpec as P

VMEM = pl.BlockSpec(memory_space=pltpu.VMEM)
SMEM = pl.BlockSpec(memory_space=pltpu.SMEM)


def joint_pairs(sizes, target):
    places = list(itertools.product(*[range(size) for size in sizes]))
    index = {place: number for number, place in enumerate(places)}
    return [(index[place], index[target(*place)]) for place in places]


def sector_product(mine, other, right, left, rows, half):
    vectors, block_rows, half_cols = mine.shape
    terms = right.shape[0]
    x_mine = mine.reshape(vectors * block_rows, half_cols)
    x_other = other.reshape(vectors * block_rows, half_cols)
    mid = []
    for term in range(terms):
        near_rows = right[term, pl.ds(pl.multiple_of(half * half_cols, half_cols), half_cols), :]
        far_rows = right[term, pl.ds(pl.multiple_of((1 - half) * half_cols, half_cols), half_cols), :]
        value = jnp.dot(x_mine, near_rows, preferred_element_type=jnp.float32)
        value = value + jnp.dot(x_other, far_rows, preferred_element_type=jnp.float32)
        mid.append(value.astype(jnp.bfloat16).reshape(vectors, block_rows, -1))
    keep = lax.broadcasted_iota(jnp.int32, (block_rows, block_rows), 1) < rows
    wide = jnp.concatenate(
        [jnp.where(keep, left[term], jnp.zeros_like(left[term])) for term in range(terms)], axis=1
    )
    out = []
    for vector in range(vectors):
        tall = jnp.concatenate([mid[term][vector] for term in range(terms)], axis=0)
        out.append(jnp.dot(wide, tall, preferred_element_type=jnp.float32))
    return out


def store_halves(values, own, send_ref, keep_ref, slot):
    own_rows = keep_ref.shape[2]
    for vector, value in enumerate(values):
        low, high = value[:own_rows], value[own_rows:]
        keep_ref[slot, vector] = jnp.where(own == 0, low, high)
        send_ref[slot, vector] = jnp.where(own == 0, high, low).astype(send_ref.dtype)


def blocks_kernel(sources, *refs):
    count = len(sources)
    rows_ref, right = refs[0], refs[1]
    blocks = refs[2:2 + 3 * count]
    send_ref, keep_ref = refs[2 + 3 * count:]
    me, own, half = lax.axis_index("sec"), lax.axis_index("ops"), lax.axis_index("sub")
    for number, (source, slot) in enumerate(sources):
        mine, other, left = blocks[3 * number:3 * number + 3]
        rows = rows_ref[me ^ source(own)]
        values = sector_product(mine[...], other[...], right, left, rows, half)
        store_halves(values, own, send_ref, keep_ref, slot(own))


def blocks_call(sources, rows, right, blocks):
    vectors, block_rows, half_cols = blocks[0].shape
    shape = (len(sources), vectors, block_rows // 2, right.shape[2])
    return pl.pallas_call(
        functools.partial(blocks_kernel, sources),
        out_shape=(
            jax.ShapeDtypeStruct(shape, jnp.bfloat16),
            jax.ShapeDtypeStruct(shape, jnp.float32),
        ),
        in_specs=[SMEM] + [VMEM] * (1 + len(blocks)),
        out_specs=(VMEM, VMEM),
        compiler_params=pltpu.CompilerParams(vmem_limit_bytes=24 << 20),
    )(rows, right, *blocks)


def final_kernel(sources, rows_ref, live_ref, *refs):
    out_ref = refs[-1]
    me, own = lax.axis_index("sec"), lax.axis_index("ops")
    vectors, own_rows, columns = out_ref.shape[0], out_ref.shape[3], out_ref.shape[4]
    row_ids = own * own_rows + lax.broadcasted_iota(jnp.int32, (own_rows, columns), 0)
    for number in range(len(sources)):
        keep_ref, got_ref = refs[2 * number], refs[2 * number + 1]
        for slot, offset in enumerate(sources[number]):
            sector = me ^ offset
            rows = jnp.where(live_ref[sector, me] > 0, rows_ref[sector], 0)
            for vector in range(vectors):
                total = keep_ref[slot, vector] + got_ref[slot, vector].astype(jnp.float32)
                total = jnp.where(row_ids < rows, total, jnp.zeros_like(total))
                out_ref[vector, sector, 0] = total.astype(out_ref.dtype)


def final_call(sources, rows, live, parts, shape):
    return pl.pallas_call(
        functools.partial(final_kernel, sources),
        out_shape=jax.ShapeDtypeStruct(shape, jnp.bfloat16),
        in_specs=[SMEM, SMEM] + [VMEM] * len(parts),
        out_specs=VMEM,
        compiler_params=pltpu.CompilerParams(vmem_limit_bytes=24 << 20),
    )(rows, live, *parts)


def local_small(psi, left_op, right_op, sector_rows, block_live):
    vectors, sec_dev, sectors, block_rows, half_cols = psi.shape
    me, own = lax.axis_index("sec"), lax.axis_index("ops")
    swap = [(0, 1), (1, 0)]
    near_pairs = [(z, z ^ 1) for z in range(4)]
    far_pairs = joint_pairs((4, 2), lambda z, o: (z ^ (2 + o), o))

    def pick(sector):
        return lax.dynamic_index_in_dim(psi[:, 0], sector, 1, keepdims=False)

    far = pick(me ^ (2 + own))
    near = pick(me ^ 1)
    mine = pick(me)
    left = left_op[:, 0]
    right = right_op[:, 0]

    far_in = lax.ppermute(far, ("sec", "ops"), far_pairs)
    left_far = lax.ppermute(left, ("sec", "sub"), far_pairs)
    near_in = lax.ppermute(near, "sec", near_pairs)
    left_near = lax.ppermute(left, "sec", near_pairs)
    mine_other = lax.ppermute(mine, "sub", swap)
    near_other = lax.ppermute(near_in, "sub", swap)
    left_far_other = lax.ppermute(left_far, "sub", swap)
    far_swapped = lax.ppermute(far_in, "ops", swap)
    far_other = lax.ppermute(far_in, "sub", swap)
    swapped_other = lax.ppermute(far_swapped, "sub", swap)

    sub = lax.axis_index("sub")
    first_left = jnp.where(sub == own, left_far, left_far_other)
    second_left = jnp.where(sub == own, left_far_other, left_far)

    send_a, keep_a = blocks_call(
        ((lambda o: 0, lambda o: 0), (lambda o: 1, lambda o: 1)),
        sector_rows, right, (mine, mine_other, left, near_in, near_other, left_near),
    )
    got_a = lax.ppermute(send_a, "ops", swap)
    send_b, keep_b = blocks_call(
        ((lambda o: 2 + o, lambda o: o), (lambda o: 3 - o, lambda o: 1 - o)),
        sector_rows, right, (far_in, far_other, first_left, far_swapped, swapped_other, second_left),
    )
    got_b = lax.ppermute(send_b, "ops", swap)
    shape = (vectors, sectors, sec_dev, block_rows // 2, right.shape[2])
    return final_call(
        ((0, 1), (2, 3)), sector_rows, block_live, (keep_a, got_a, keep_b, got_b), shape
    )


def local_any(psi, left_op, right_op, sector_rows, block_live):
    vectors, sec_dev, sectors, block_rows, half_cols = psi.shape
    terms = left_op.shape[0]
    own_rows = block_rows // lax.axis_size("ops")
    sec_start = lax.axis_index("sec") * sec_dev
    row_ids = lax.broadcasted_iota(jnp.int32, (sectors, block_rows), 1)
    row_keep = row_ids < sector_rows[:, None]
    live_right = lax.dynamic_slice_in_dim(block_live, sec_start, sec_dev, 1)
    keep_right = row_keep[:, None, :, None] & (live_right[:, :, None, None] > 0)
    empty = jnp.zeros((vectors, sectors, sec_dev, block_rows, half_cols), jnp.float32)
    moved = lax.all_to_all(psi, "sec", split_axis=2, concat_axis=1, tiled=True)
    moved = jnp.where(keep_right[None], moved, jnp.zeros_like(moved))
    lefts = lax.all_gather(left_op, "sec", axis=1, tiled=True)
    piece = lax.all_gather(moved, "sub", axis=4, tiled=True)

    def one_term(index, acc):
        mid = jnp.einsum(
            "vacjk,ckl->vacjl", piece, right_op[index], preferred_element_type=jnp.float32
        ).astype(jnp.bfloat16)
        return acc + jnp.einsum(
            "aij,vacjl->vacil", lefts[index], mid, preferred_element_type=jnp.float32
        )

    partial_value = lax.fori_loop(0, terms, one_term, empty)
    summed = lax.psum(partial_value.astype(jnp.bfloat16), "ops").astype(jnp.float32)
    own = lax.dynamic_slice_in_dim(summed, lax.axis_index("ops") * own_rows, own_rows, 3)
    keep_own = lax.dynamic_slice_in_dim(keep_right, lax.axis_index("ops") * own_rows, own_rows, 2)
    total = jnp.where(keep_own[None], own, jnp.zeros_like(own))
    return total.astype(jnp.bfloat16)


def solution(mesh):
    sizes = dict(mesh.shape)
    small = sizes["sec"] == 4 and sizes["ops"] == 2 and sizes["sub"] == 2
    return jax.shard_map(
        local_small if small else local_any,
        mesh=mesh,
        in_specs=(
            P("runs", "sec", None, None, "sub"),
            P(("runs", "ops"), "sec", None, None),
            P(("runs", "ops"), "sec", None, "sub"),
            P("runs"),
            P("runs", None),
        ),
        out_specs=P("runs", None, "sec", "ops", "sub"),
        check_vma=False,
    )
```

```python
import functools

import jax
import jax.numpy as jnp
from jax import lax
from jax.experimental import pallas as pl
from jax.experimental.pallas import tpu as pltpu
from jax.sharding import PartitionSpec as P

VMEM = pl.BlockSpec(memory_space=pltpu.VMEM)
SMEM = pl.BlockSpec(memory_space=pltpu.SMEM)


def wide_left(low, high, rows):
    wide = jnp.concatenate([low, high], axis=1)
    block_rows = wide.shape[0]
    column = lax.broadcasted_iota(jnp.int32, wide.shape, 1) % block_rows
    return jnp.where(column < rows, wide, jnp.zeros_like(wide))


def sector_product(mine, other, right, wide, half):
    vectors, block_rows, half_cols = mine.shape
    terms = right.shape[0]
    x_mine = mine.reshape(vectors * block_rows, half_cols)
    x_other = other.reshape(vectors * block_rows, half_cols)
    mid = []
    for term in range(terms):
        near_rows = right[term, pl.ds(pl.multiple_of(half * half_cols, half_cols), half_cols), :]
        far_rows = right[term, pl.ds(pl.multiple_of((1 - half) * half_cols, half_cols), half_cols), :]
        value = jnp.dot(x_mine, near_rows, preferred_element_type=jnp.float32)
        value = value + jnp.dot(x_other, far_rows, preferred_element_type=jnp.float32)
        mid.append(value.astype(jnp.bfloat16).reshape(vectors, block_rows, -1))
    out = []
    for vector in range(vectors):
        tall = jnp.concatenate([mid[term][vector] for term in range(terms)], axis=0)
        out.append(jnp.dot(wide, tall, preferred_element_type=jnp.float32))
    return out


def store_halves(values, own, send_ref, keep_ref, slot):
    own_rows = keep_ref.shape[2]
    for vector, value in enumerate(values):
        low, high = value[:own_rows], value[own_rows:]
        keep_ref[slot, vector] = jnp.where(own == 0, low, high)
        send_ref[slot, vector] = jnp.where(own == 0, high, low).astype(send_ref.dtype)


def halves(mine, other, half):
    return jnp.where(half == 0, mine, other), jnp.where(half == 0, other, mine)


def by_vector(values, own):
    return jnp.where(own == 0, values[0], values[1]), jnp.where(own == 0, values[1], values[0])


def own_kernel(rows_ref, live_ref, right, left, mine, other, send_ref, keep_ref, used_ref, shown_ref):
    me, own, half = lax.axis_index("sec"), lax.axis_index("ops"), lax.axis_index("sub")
    sectors = rows_ref.shape[0]
    for offset in range(sectors):
        sector = me ^ offset
        used = rows_ref[sector]
        used_ref[offset] = jnp.full(used_ref.shape[1:], used, jnp.int32)
        shown_ref[offset] = jnp.full(
            shown_ref.shape[1:], jnp.where(live_ref[sector, me] > 0, used, 0), jnp.int32
        )
    low = jnp.concatenate([left[0], left[1]], axis=1)
    high = jnp.concatenate([left[2], left[3]], axis=1)
    values = sector_product(mine[...], other[...], right, wide_left(low, high, rows_ref[me]), half)
    store_halves(values, own, send_ref, keep_ref, 0)


def near_kernel(used_ref, right, near, other, send_ref, keep_ref):
    own, half = lax.axis_index("ops"), lax.axis_index("sub")
    wide = wide_left(*halves(near[2], other[2], half), used_ref[1, :1, :1])
    values = sector_product(near[:2], other[:2], right, wide, half)
    store_halves(values, own, send_ref, keep_ref, 0)


def early_kernel(rows_ref, live_ref, right, left, mine, other, near, near_other,
                 send_ref, keep_ref, used_ref, shown_ref):
    own_kernel(rows_ref, live_ref, right, left, mine, other, send_ref.at[:1], keep_ref.at[:1], used_ref, shown_ref)
    near_kernel(used_ref, right, near, near_other, send_ref.at[1:], keep_ref.at[1:])


def far_kernel(plan, used_ref, right, *refs):
    own, half = lax.axis_index("ops"), lax.axis_index("sub")
    send_ref, keep_ref = refs[-2:]
    for number, (offset, own_order) in enumerate(plan):
        psi, other, left, left_other = refs[4 * number:4 * number + 4]
        wide = wide_left(*halves(left[0], left_other[0], half), used_ref[offset, :1, :1])
        values = sector_product(psi[:2], other[:2], right, wide, half)
        if own_order:
            values = by_vector(values, own)
        store_halves(values, own, send_ref, keep_ref, number)


PARAMS = pltpu.CompilerParams(vmem_limit_bytes=24 << 20)


def cost(us):
    return pl.CostEstimate(flops=int(us * 1.15e9), bytes_accessed=0, transcendentals=0)


def blocks_call(kernel, count, right, *operands, scalars=(), extra=(), us=0):
    columns = right.shape[2]
    shape = (count, 2, right.shape[1] // 8, columns)
    return pl.pallas_call(
        kernel,
        out_shape=(
            jax.ShapeDtypeStruct(shape, jnp.bfloat16),
            jax.ShapeDtypeStruct(shape, jnp.float32),
            *extra,
        ),
        in_specs=[SMEM] * len(scalars) + [VMEM] * (len(operands)),
        out_specs=(VMEM,) * (2 + len(extra)),
        cost_estimate=cost(us),
        compiler_params=PARAMS,
    )(*scalars, *operands)


def final_kernel(shown_ref, keep_m, got_m, keep_n, got_n, keep_b, got_b, keep_c, got_c, out_ref):
    me, own = lax.axis_index("sec"), lax.axis_index("ops")
    vectors, own_rows, columns = out_ref.shape[0], out_ref.shape[3], out_ref.shape[4]
    row_ids = own * own_rows + lax.broadcasted_iota(jnp.int32, (own_rows, columns), 0)
    pairs = (
        (0, keep_m.at[0], got_m.at[0]), (1, keep_n.at[0], got_n.at[0]),
        (3, keep_b.at[0], got_b.at[0]), (2, keep_c.at[0], got_c.at[0]),
    )
    for offset, keep_ref, got_ref in pairs:
        keep = row_ids < shown_ref[offset, :1, :1]
        for vector in range(vectors):
            total = keep_ref[vector] + got_ref[vector].astype(jnp.float32)
            total = jnp.where(keep, total, jnp.zeros_like(total))
            out_ref[vector, me ^ offset, 0] = total.astype(out_ref.dtype)


def final_call(shown, parts, shape):
    return pl.pallas_call(
        final_kernel,
        out_shape=jax.ShapeDtypeStruct(shape, jnp.bfloat16),
        in_specs=[VMEM] * (1 + len(parts)),
        out_specs=VMEM,
        cost_estimate=cost(0),
        compiler_params=PARAMS,
    )(shown, *parts)


def local_small(psi, left_op, right_op, sector_rows, block_live):
    vectors, sec_dev, sectors, block_rows, half_cols = psi.shape
    me, own, half = lax.axis_index("sec"), lax.axis_index("ops"), lax.axis_index("sub")
    right, left = right_op[:, 0], left_op[:, 0]
    swap = [(0, 1), (1, 0)]

    def exchange(value, offset):
        return lax.ppermute(value, "sec", [(z, z ^ offset) for z in range(sectors)])

    def in_pieces(value, axis_name, count):
        if count == 1:
            return lax.ppermute(value, axis_name, swap)
        flat = value.reshape(-1, value.shape[-1])
        parts = jnp.split(flat, count)
        return jnp.concatenate([lax.ppermute(part, axis_name, swap) for part in parts]).reshape(value.shape)

    def other_core(value, count=1):
        return in_pieces(value, "sub", count)

    def pick(vector, offset):
        block = lax.dynamic_slice(
            psi, (vector, 0, me ^ offset, 0, 0), (1, 1, 1, block_rows, half_cols)
        )
        return block.reshape(1, block_rows, half_cols)

    pieces = [pick(0, 0), pick(1, 0), pick(0, 1), pick(1, 1), pick(0, 2), pick(1, 2), pick(own, 3)]
    left_late, *pieces = lax.optimization_barrier((left, *pieces))
    half_left = lax.dynamic_slice_in_dim(left_late, half * 2, 2, 0)
    half_left = jnp.concatenate([half_left[0], half_left[1]], axis=1)[None]
    mine = jnp.concatenate(pieces[:2])
    near = jnp.concatenate([*pieces[2:4], half_left])
    skip = jnp.concatenate([*pieces[4:6], half_left])
    cross = jnp.concatenate([*pieces[6:], half_left])
    rows_shape = jax.ShapeDtypeStruct((sectors, 8, 128), jnp.int32)
    near_in = exchange(near, 1)
    cross_in = exchange(cross, 3)
    skip_in = exchange(skip, 2)
    mine_other = other_core(mine, 2)
    near_other = other_core(near_in, 3)
    send_a, keep_a, used, shown = blocks_call(early_kernel, 2, right, right, left, mine, mine_other, near_in, near_other, scalars=(sector_rows, block_live), extra=(rows_shape, rows_shape), us=0)
    got_a = in_pieces(send_a, "ops", 2)
    cross_left = cross_in[1:]
    cross_swapped = in_pieces(cross_in[:1], "ops", 1)
    cross_swapped, got_a = lax.optimization_barrier((cross_swapped, got_a))
    cross_psi = jnp.concatenate([cross_in[:1], cross_swapped])
    cross_other = other_core(cross_psi, 2)
    cross_left_other = other_core(cross_left, 1)
    send_b, keep_b = blocks_call(functools.partial(far_kernel, ((3, True),)), 1, right, used, right, cross_psi, cross_other, cross_left, cross_left_other, us=0)
    got_b = in_pieces(send_b, "ops", 1)
    skip_in, send_b = lax.optimization_barrier((skip_in, send_b))
    skip_other = other_core(skip_in, 3)
    skip_left, skip_left_other = skip_in[2:], skip_other[2:]
    send_c, keep_c = blocks_call(functools.partial(far_kernel, ((2, False),)), 1, right, used, right, skip_in, skip_other, skip_left, skip_left_other, us=0)
    got_c = in_pieces(send_c, "ops", 1)
    keep_m, keep_n, got_m, got_n = keep_a[:1], keep_a[1:], got_a[:1], got_a[1:]
    shape = (vectors, sectors, sec_dev, block_rows // 2, half_cols)
    return final_call(shown, (keep_m, got_m, keep_n, got_n, keep_b, got_b, keep_c, got_c), shape)


def local_any(psi, left_op, right_op, sector_rows, block_live):
    vectors, sec_dev, sectors, block_rows, half_cols = psi.shape
    terms = left_op.shape[0]
    own_rows = block_rows // lax.axis_size("ops")
    sec_start = lax.axis_index("sec") * sec_dev
    row_ids = lax.broadcasted_iota(jnp.int32, (sectors, block_rows), 1)
    row_keep = row_ids < sector_rows[:, None]
    live_right = lax.dynamic_slice_in_dim(block_live, sec_start, sec_dev, 1)
    keep_right = row_keep[:, None, :, None] & (live_right[:, :, None, None] > 0)
    empty = jnp.zeros((vectors, sectors, sec_dev, block_rows, half_cols), jnp.float32)
    moved = lax.all_to_all(psi, "sec", split_axis=2, concat_axis=1, tiled=True)
    moved = jnp.where(keep_right[None], moved, jnp.zeros_like(moved))
    lefts = lax.all_gather(left_op, "sec", axis=1, tiled=True)
    piece = lax.all_gather(moved, "sub", axis=4, tiled=True)

    def one_term(index, acc):
        mid = jnp.einsum(
            "vacjk,ckl->vacjl", piece, right_op[index], preferred_element_type=jnp.float32
        ).astype(jnp.bfloat16)
        return acc + jnp.einsum(
            "aij,vacjl->vacil", lefts[index], mid, preferred_element_type=jnp.float32
        )

    partial_value = lax.fori_loop(0, terms, one_term, empty)
    summed = lax.psum(partial_value.astype(jnp.bfloat16), "ops").astype(jnp.float32)
    own = lax.dynamic_slice_in_dim(summed, lax.axis_index("ops") * own_rows, own_rows, 3)
    keep_own = lax.dynamic_slice_in_dim(keep_right, lax.axis_index("ops") * own_rows, own_rows, 2)
    total = jnp.where(keep_own[None], own, jnp.zeros_like(own))
    return total.astype(jnp.bfloat16)


def solution(mesh):
    sizes = dict(mesh.shape)
    small = sizes["sec"] == 4 and sizes["ops"] == 2 and sizes["sub"] == 2
    return jax.shard_map(
        local_small if small else local_any,
        mesh=mesh,
        in_specs=(
            P("runs", "sec", None, None, "sub"),
            P(("runs", "ops"), "sec", None, None),
            P(("runs", "ops"), "sec", None, "sub"),
            P("runs"),
            P("runs", None),
        ),
        out_specs=P("runs", None, "sec", "ops", "sub"),
        check_vma=False,
    )
```

```python
import functools

import jax
import jax.numpy as jnp
from jax import lax
from jax.experimental import pallas as pl
from jax.experimental.pallas import tpu as pltpu
from jax.sharding import PartitionSpec as P

VMEM = pl.BlockSpec(memory_space=pltpu.VMEM)


def wide_left(low, high, rows):
    wide = jnp.concatenate([low, high], axis=1)
    block_rows = wide.shape[0]
    column = lax.broadcasted_iota(jnp.int32, wide.shape, 1) % block_rows
    return jnp.where(column < rows, wide, jnp.zeros_like(wide))


def right_product(mine, other, right, half):
    vectors, block_rows, half_cols = mine.shape
    terms = right.shape[0]
    x_mine = mine.reshape(vectors * block_rows, half_cols)
    x_other = other.reshape(vectors * block_rows, half_cols)
    mid = []
    for term in range(terms):
        near_rows = right[term, pl.ds(pl.multiple_of(half * half_cols, half_cols), half_cols), :]
        far_rows = right[term, pl.ds(pl.multiple_of((1 - half) * half_cols, half_cols), half_cols), :]
        value = jnp.dot(x_mine, near_rows, preferred_element_type=jnp.float32)
        value = value + jnp.dot(x_other, far_rows, preferred_element_type=jnp.float32)
        mid.append(value.astype(jnp.bfloat16).reshape(vectors, block_rows, -1))
    return [
        jnp.concatenate([mid[term][vector] for term in range(terms)], axis=0) for vector in range(vectors)
    ]


def left_product(wide, tall):
    return [jnp.dot(wide, value, preferred_element_type=jnp.float32) for value in tall]


def store_halves(values, own, send_ref, keep_ref, slot):
    own_rows = keep_ref.shape[2]
    for vector, value in enumerate(values):
        low, high = value[:own_rows], value[own_rows:]
        keep_ref[slot, vector] = jnp.where(own == 0, low, high)
        send_ref[slot, vector] = jnp.where(own == 0, high, low).astype(send_ref.dtype)


def halves(mine, other, half):
    return jnp.where(half == 0, mine, other), jnp.where(half == 0, other, mine)


def by_vector(values, own):
    return jnp.where(own == 0, values[0], values[1]), jnp.where(own == 0, values[1], values[0])


def own_kernel(rows_hbm, live_hbm, right, left, mine, other,
               send_ref, keep_ref, used_ref, shown_ref, rows_ref, live_ref, sems):
    me, own, half = lax.axis_index("sec"), lax.axis_index("ops"), lax.axis_index("sub")
    copies = [
        pltpu.make_async_copy(rows_hbm, rows_ref, sems.at[0]),
        pltpu.make_async_copy(live_hbm, live_ref, sems.at[1]),
    ]
    for copy in copies:
        copy.start()
    tall = right_product(mine[...], other[...], right, half)
    for copy in copies:
        copy.wait()
    for offset in range(rows_ref.shape[0]):
        sector = me ^ offset
        used = rows_ref[sector]
        used_ref[offset] = jnp.full(used_ref.shape[1:], used, jnp.int32)
        shown_ref[offset] = jnp.full(
            shown_ref.shape[1:], jnp.where(live_ref[sector, me] > 0, used, 0), jnp.int32
        )
    low = jnp.concatenate([left[0], left[1]], axis=1)
    high = jnp.concatenate([left[2], left[3]], axis=1)
    values = left_product(wide_left(low, high, rows_ref[me]), tall)
    store_halves(values, own, send_ref, keep_ref, 0)


def block_kernel(plan, used_ref, right, *refs):
    own, half = lax.axis_index("ops"), lax.axis_index("sub")
    send_ref, keep_ref = refs[-2:]
    for number, (offset, own_order) in enumerate(plan):
        psi, other, left, left_other = refs[4 * number:4 * number + 4]
        tall = right_product(psi[:2], other[:2], right, half)
        if left.shape[0] == 1:
            sides = halves(left[0], left_other[0], half)
        else:
            whole = [jnp.where(half == offset - 2, left[term], left_other[term]) for term in range(4)]
            sides = jnp.concatenate(whole[:2], axis=1), jnp.concatenate(whole[2:], axis=1)
        wide = wide_left(*sides, used_ref[offset, :1, :1])
        values = left_product(wide, tall)
        if own_order:
            values = by_vector(values, own)
        store_halves(values, own, send_ref, keep_ref, number)


PARAMS = pltpu.CompilerParams(vmem_limit_bytes=24 << 20)


def cost(us):
    return pl.CostEstimate(flops=int(us * 1.15e9), bytes_accessed=0, transcendentals=0)


def blocks_call(kernel, count, right, *operands, scalars=(), extra=(), us=0):
    shape = (count, 2, right.shape[1] // 8, right.shape[2])
    scratch = [pltpu.SMEM(array.shape, array.dtype) for array in scalars]
    if scalars:
        scratch.append(pltpu.SemaphoreType.DMA((len(scalars),)))
    return pl.pallas_call(
        kernel,
        out_shape=(
            jax.ShapeDtypeStruct(shape, jnp.bfloat16),
            jax.ShapeDtypeStruct(shape, jnp.float32),
            *extra,
        ),
        in_specs=[pl.BlockSpec(memory_space=pltpu.HBM)] * len(scalars) + [VMEM] * len(operands),
        out_specs=(VMEM,) * (2 + len(extra)),
        scratch_shapes=scratch,
        cost_estimate=cost(us),
        compiler_params=PARAMS,
    )(*scalars, *operands)


def final_kernel(shown_ref, keep_m, got_m, keep_n, got_n, keep_b, got_b, keep_c, got_c, out_ref):
    me, own = lax.axis_index("sec"), lax.axis_index("ops")
    vectors, own_rows, columns = out_ref.shape[0], out_ref.shape[3], out_ref.shape[4]
    row_ids = own * own_rows + lax.broadcasted_iota(jnp.int32, (own_rows, columns), 0)
    pairs = (
        (0, keep_m.at[0], got_m.at[0]), (1, keep_n.at[0], got_n.at[0]),
        (3, keep_b.at[0], got_b.at[0]), (2, keep_c.at[0], got_c.at[0]),
    )
    for offset, keep_ref, got_ref in pairs:
        keep = row_ids < shown_ref[offset, :1, :1]
        for vector in range(vectors):
            total = keep_ref[vector] + got_ref[vector].astype(jnp.float32)
            total = jnp.where(keep, total, jnp.zeros_like(total))
            out_ref[vector, me ^ offset, 0] = total.astype(out_ref.dtype)


def final_call(shown, parts, shape):
    return pl.pallas_call(
        final_kernel,
        out_shape=jax.ShapeDtypeStruct(shape, jnp.bfloat16),
        in_specs=[VMEM] * (1 + len(parts)),
        out_specs=VMEM,
        cost_estimate=cost(0),
        compiler_params=PARAMS,
    )(shown, *parts)


def local_small(psi, left_op, right_op, sector_rows, block_live):
    vectors, sec_dev, sectors, block_rows, half_cols = psi.shape
    me, own, half = lax.axis_index("sec"), lax.axis_index("ops"), lax.axis_index("sub")
    right, left = right_op[:, 0], left_op[:, 0]
    swap = [(0, 1), (1, 0)]

    def exchange(value, offset):
        return lax.ppermute(value, "sec", [(z, z ^ offset) for z in range(sectors)])

    def in_pieces(value, axis_name, count):
        if count == 1:
            return lax.ppermute(value, axis_name, swap)
        flat = value.reshape(-1, value.shape[-1])
        parts = jnp.split(flat, count)
        return jnp.concatenate([lax.ppermute(part, axis_name, swap) for part in parts]).reshape(value.shape)

    def other_core(value, count=1):
        return in_pieces(value, "sub", count)

    def pick(vector, offset):
        block = lax.dynamic_slice(
            psi, (vector, 0, me ^ offset, 0, 0), (1, 1, 1, block_rows, half_cols)
        )
        return block.reshape(1, block_rows, half_cols)

    pieces = [pick(0, 0), pick(1, 0), pick(0, 1), pick(1, 1), pick(0, 2), pick(1, 2), pick(own, 3)]
    left_late, *pieces = lax.optimization_barrier((left, *pieces))
    half_left = lax.dynamic_slice_in_dim(left_late, half * 2, 2, 0)
    half_left = jnp.concatenate([half_left[0], half_left[1]], axis=1)[None]
    mine = jnp.concatenate(pieces[:2])
    near = jnp.concatenate([*pieces[2:4], half_left])
    skip = jnp.concatenate([*pieces[4:6]])
    cross = jnp.concatenate([*pieces[6:]])
    rows_shape = jax.ShapeDtypeStruct((sectors, 8, 128), jnp.int32)
    far_pairs = [(2 * z + s, 2 * (z ^ (2 + s)) + s) for z in range(4) for s in range(2)]
    cross_left = skip_left = lax.ppermute(left, ("sec", "sub"), far_pairs)
    near_in = exchange(near, 1)
    cross_in = exchange(cross, 3)
    skip_in = exchange(skip, 2)
    cross_left_other = skip_left_other = in_pieces(cross_left, "sub", 1)
    mine_other = other_core(mine, 1)
    near_other = other_core(near_in, 2)
    send_m, keep_m, used, shown = blocks_call(own_kernel, 1, right, right, left, mine, mine_other, scalars=(sector_rows, block_live), extra=(rows_shape, rows_shape), us=0)
    send_n, keep_n = blocks_call(functools.partial(block_kernel, ((1, False),)), 1, right, used, right, near_in, near_other, near_in[2:], near_other[2:], us=0)
    got_m = in_pieces(send_m, "ops", 2)
    got_n = in_pieces(send_n, "ops", 1)
    cross_in, got_m = lax.optimization_barrier((cross_in, got_m))
    cross_swapped = in_pieces(cross_in[:1], "ops", 1)
    cross_psi = jnp.concatenate([cross_in[:1], cross_swapped])
    cross_other = other_core(cross_psi, 2)
    send_b, keep_b = blocks_call(functools.partial(block_kernel, ((3, True),)), 1, right, used, right, cross_psi, cross_other, cross_left, cross_left_other, us=0)
    got_b = in_pieces(send_b, "ops", 1)
    skip_in, send_b = lax.optimization_barrier((skip_in, send_b))
    skip_other = other_core(skip_in, 1)
    send_c, keep_c = blocks_call(functools.partial(block_kernel, ((2, False),)), 1, right, used, right, skip_in, skip_other, skip_left, skip_left_other, us=0)
    got_c = in_pieces(send_c, "ops", 1)
    shape = (vectors, sectors, sec_dev, block_rows // 2, half_cols)
    return final_call(shown, (keep_m, got_m, keep_n, got_n, keep_b, got_b, keep_c, got_c), shape)


def local_any(psi, left_op, right_op, sector_rows, block_live):
    vectors, sec_dev, sectors, block_rows, half_cols = psi.shape
    terms = left_op.shape[0]
    own_rows = block_rows // lax.axis_size("ops")
    sec_start = lax.axis_index("sec") * sec_dev
    row_ids = lax.broadcasted_iota(jnp.int32, (sectors, block_rows), 1)
    row_keep = row_ids < sector_rows[:, None]
    live_right = lax.dynamic_slice_in_dim(block_live, sec_start, sec_dev, 1)
    keep_right = row_keep[:, None, :, None] & (live_right[:, :, None, None] > 0)
    empty = jnp.zeros((vectors, sectors, sec_dev, block_rows, half_cols), jnp.float32)
    moved = lax.all_to_all(psi, "sec", split_axis=2, concat_axis=1, tiled=True)
    moved = jnp.where(keep_right[None], moved, jnp.zeros_like(moved))
    lefts = lax.all_gather(left_op, "sec", axis=1, tiled=True)
    piece = lax.all_gather(moved, "sub", axis=4, tiled=True)

    def one_term(index, acc):
        mid = jnp.einsum(
            "vacjk,ckl->vacjl", piece, right_op[index], preferred_element_type=jnp.float32
        ).astype(jnp.bfloat16)
        return acc + jnp.einsum(
            "aij,vacjl->vacil", lefts[index], mid, preferred_element_type=jnp.float32
        )

    partial_value = lax.fori_loop(0, terms, one_term, empty)
    summed = lax.psum(partial_value.astype(jnp.bfloat16), "ops").astype(jnp.float32)
    own = lax.dynamic_slice_in_dim(summed, lax.axis_index("ops") * own_rows, own_rows, 3)
    keep_own = lax.dynamic_slice_in_dim(keep_right, lax.axis_index("ops") * own_rows, own_rows, 2)
    total = jnp.where(keep_own[None], own, jnp.zeros_like(own))
    return total.astype(jnp.bfloat16)


def solution(mesh):
    sizes = dict(mesh.shape)
    small = sizes["sec"] == 4 and sizes["ops"] == 2 and sizes["sub"] == 2
    return jax.shard_map(
        local_small if small else local_any,
        mesh=mesh,
        in_specs=(
            P("runs", "sec", None, None, "sub"),
            P(("runs", "ops"), "sec", None, None),
            P(("runs", "ops"), "sec", None, "sub"),
            P("runs"),
            P("runs", None),
        ),
        out_specs=P("runs", None, "sec", "ops", "sub"),
        check_vma=False,
    )
```

```python
import functools

import jax
import jax.numpy as jnp
from jax import lax
from jax.experimental import pallas as pl
from jax.experimental.pallas import tpu as pltpu
from jax.sharding import PartitionSpec as P

VMEM = pl.BlockSpec(memory_space=pltpu.VMEM)


def wide_left(low, high, rows):
    wide = jnp.concatenate([low, high], axis=1)
    block_rows = wide.shape[0]
    column = lax.broadcasted_iota(jnp.int32, wide.shape, 1) % block_rows
    return jnp.where(column < rows, wide, jnp.zeros_like(wide))


def right_product(mine, other, right, half):
    vectors, block_rows, half_cols = mine.shape
    terms = right.shape[0]
    x_mine = mine.reshape(vectors * block_rows, half_cols)
    x_other = other.reshape(vectors * block_rows, half_cols)
    mid = []
    for term in range(terms):
        near_rows = right[term, pl.ds(pl.multiple_of(half * half_cols, half_cols), half_cols), :]
        far_rows = right[term, pl.ds(pl.multiple_of((1 - half) * half_cols, half_cols), half_cols), :]
        value = jnp.dot(x_mine, near_rows, preferred_element_type=jnp.float32)
        value = value + jnp.dot(x_other, far_rows, preferred_element_type=jnp.float32)
        mid.append(value.astype(jnp.bfloat16).reshape(vectors, block_rows, -1))
    return [
        jnp.concatenate([mid[term][vector] for term in range(terms)], axis=0) for vector in range(vectors)
    ]


def left_product(wide, tall):
    return [jnp.dot(wide, value, preferred_element_type=jnp.float32) for value in tall]


def store_halves(values, own, send_ref, keep_ref, slot):
    own_rows = keep_ref.shape[2]
    for vector, value in enumerate(values):
        low, high = value[:own_rows], value[own_rows:]
        keep_ref[slot, vector] = jnp.where(own == 0, low, high)
        send_ref[slot, vector] = jnp.where(own == 0, high, low).astype(send_ref.dtype)


def halves(mine, other, half):
    return jnp.where(half == 0, mine, other), jnp.where(half == 0, other, mine)


def own_kernel(rows_hbm, live_hbm, right, left, mine, other,
               send_ref, keep_ref, used_ref, shown_ref, rows_ref, live_ref, sems):
    me, own, half = lax.axis_index("sec"), lax.axis_index("ops"), lax.axis_index("sub")
    copies = [
        pltpu.make_async_copy(rows_hbm, rows_ref, sems.at[0]),
        pltpu.make_async_copy(live_hbm, live_ref, sems.at[1]),
    ]
    for copy in copies:
        copy.start()
    tall = right_product(mine[...], other[...], right, half)
    for copy in copies:
        copy.wait()
    for offset in range(rows_ref.shape[0]):
        sector = me ^ offset
        used = rows_ref[sector]
        used_ref[offset] = jnp.full(used_ref.shape[1:], used, jnp.int32)
        shown_ref[offset] = jnp.full(
            shown_ref.shape[1:], jnp.where(live_ref[sector, me] > 0, used, 0), jnp.int32
        )
    low = jnp.concatenate([left[0], left[1]], axis=1)
    high = jnp.concatenate([left[2], left[3]], axis=1)
    values = left_product(wide_left(low, high, rows_ref[me]), tall)
    store_halves(values, own, send_ref, keep_ref, 0)


def near_kernel(used_ref, right, near, other, send_ref, keep_ref):
    own, half = lax.axis_index("ops"), lax.axis_index("sub")
    tall = right_product(near[:2], other[:2], right, half)
    wide = wide_left(*halves(near[2], other[2], half), used_ref[1, :1, :1])
    store_halves(left_product(wide, tall), own, send_ref, keep_ref, 0)


def far_kernel(place, used_ref, right, psi, other, left, left_other, send_ref, keep_ref):
    own, half = lax.axis_index("ops"), lax.axis_index("sub")
    number = jnp.where(own == place, 0, 1)
    tall = right_product(psi[...], other[...], right, half)
    whole = [jnp.where(half == number, left[term], left_other[term]) for term in range(left.shape[0])]
    sides = jnp.concatenate(whole[:2], axis=1), jnp.concatenate(whole[2:], axis=1)
    wide = wide_left(*sides, used_ref[2 + number, :1, :1])
    store_halves(left_product(wide, tall), own, send_ref, keep_ref, 0)


PARAMS = pltpu.CompilerParams(vmem_limit_bytes=24 << 20)


def cost(us):
    return pl.CostEstimate(flops=int(us * 1.15e9), bytes_accessed=0, transcendentals=0)


def blocks_call(kernel, count, right, *operands, scalars=(), extra=(), us=0):
    shape = (count, 2, right.shape[1] // 8, right.shape[2])
    scratch = [pltpu.SMEM(array.shape, array.dtype) for array in scalars]
    if scalars:
        scratch.append(pltpu.SemaphoreType.DMA((len(scalars),)))
    return pl.pallas_call(
        kernel,
        out_shape=(
            jax.ShapeDtypeStruct(shape, jnp.bfloat16),
            jax.ShapeDtypeStruct(shape, jnp.float32),
            *extra,
        ),
        in_specs=[pl.BlockSpec(memory_space=pltpu.HBM)] * len(scalars) + [VMEM] * len(operands),
        out_specs=(VMEM,) * (2 + len(extra)),
        scratch_shapes=scratch,
        cost_estimate=cost(us),
        compiler_params=PARAMS,
    )(*scalars, *operands)


def final_kernel(shown_ref, keep_m, got_m, keep_n, got_n, keep_b, got_b, keep_c, got_c, out_ref):
    me, own = lax.axis_index("sec"), lax.axis_index("ops")
    vectors, own_rows, columns = out_ref.shape[0], out_ref.shape[3], out_ref.shape[4]
    row_ids = own * own_rows + lax.broadcasted_iota(jnp.int32, (own_rows, columns), 0)
    pairs = (
        (0, keep_m.at[0], got_m.at[0]), (1, keep_n.at[0], got_n.at[0]),
        (2 + own, keep_b.at[0], got_c.at[0]), (3 - own, keep_c.at[0], got_b.at[0]),
    )
    for offset, keep_ref, got_ref in pairs:
        shown = row_ids < shown_ref[offset, :1, :1]
        for vector in range(vectors):
            total = keep_ref[vector] + got_ref[vector].astype(jnp.float32)
            total = jnp.where(shown, total, jnp.zeros_like(total))
            out_ref[vector, me ^ offset, 0] = total.astype(out_ref.dtype)


def final_call(shown, parts, shape):
    return pl.pallas_call(
        final_kernel,
        out_shape=jax.ShapeDtypeStruct(shape, jnp.bfloat16),
        in_specs=[VMEM] * (1 + len(parts)),
        out_specs=VMEM,
        cost_estimate=cost(0),
        compiler_params=PARAMS,
    )(shown, *parts)


def local_small(psi, left_op, right_op, sector_rows, block_live):
    vectors, sec_dev, sectors, block_rows, half_cols = psi.shape
    me, own, half = lax.axis_index("sec"), lax.axis_index("ops"), lax.axis_index("sub")
    right, left = right_op[:, 0], left_op[:, 0]
    swap = [(0, 1), (1, 0)]

    def exchange(value, offset):
        return lax.ppermute(value, "sec", [(z, z ^ offset) for z in range(sectors)])

    def in_pieces(value, axis_name, count):
        if count == 1:
            return lax.ppermute(value, axis_name, swap)
        flat = value.reshape(-1, value.shape[-1])
        parts = jnp.split(flat, count)
        return jnp.concatenate([lax.ppermute(part, axis_name, swap) for part in parts]).reshape(value.shape)

    def other_core(value, count=1):
        return in_pieces(value, "sub", count)

    def pick(vector, offset):
        block = lax.dynamic_slice(
            psi, (vector, 0, me ^ offset, 0, 0), (1, 1, 1, block_rows, half_cols)
        )
        return block.reshape(1, block_rows, half_cols)

    pieces = [pick(vector, offset) for offset in (0, 1, 2 + own) for vector in range(vectors)]
    left_late, *pieces = lax.optimization_barrier((left, *pieces))
    half_left = lax.dynamic_slice_in_dim(left_late, half * 2, 2, 0)
    half_left = jnp.concatenate([half_left[0], half_left[1]], axis=1)[None]
    mine = jnp.concatenate(pieces[:2])
    near = jnp.concatenate([*pieces[2:4], half_left])
    far = jnp.concatenate(pieces[4:])

    def cross(size):
        return [(2 * z + p, 2 * (z ^ (2 + p)) + p) for z in range(sectors) for p in range(size)]

    rows_shape = jax.ShapeDtypeStruct((sectors, 8, 128), jnp.int32)
    left_far = lax.ppermute(left, ("sec", "sub"), cross(2))
    far_in = lax.ppermute(far, ("sec", "ops"), cross(2))
    near_in = exchange(near, 1)
    mine_other = other_core(mine, 1)
    near_other = other_core(near_in, 2)
    left_far_other = in_pieces(left_far, "sub", 2)
    send_m, keep_m, used, shown = blocks_call(own_kernel, 1, right, right, left, mine, mine_other, scalars=(sector_rows, block_live), extra=(rows_shape, rows_shape), us=0)
    send_n, keep_n = blocks_call(near_kernel, 1, right, used, right, near_in, near_other, us=5)
    got_m = in_pieces(send_m, "ops", 1)
    got_n = in_pieces(send_n, "ops", 1)
    far_in, got_m = lax.optimization_barrier((far_in, got_m))
    far_swapped = in_pieces(far_in, "ops", 1)
    far_other = other_core(far_in, 2)
    send_b, keep_b = blocks_call(functools.partial(far_kernel, 0), 1, right, used, right, far_in, far_other, left_far, left_far_other, us=2)
    got_b = lax.ppermute(send_b, "ops", swap)
    far_swapped, send_b = lax.optimization_barrier((far_swapped, send_b))
    swapped_other = other_core(far_swapped, 1)
    send_c, keep_c = blocks_call(functools.partial(far_kernel, 1), 1, right, used, right, far_swapped, swapped_other, left_far, left_far_other, us=0)
    got_c = lax.ppermute(send_c, "ops", swap)
    shape = (vectors, sectors, sec_dev, block_rows // 2, half_cols)
    return final_call(shown, (keep_m, got_m, keep_n, got_n, keep_b, got_b, keep_c, got_c), shape)


def local_any(psi, left_op, right_op, sector_rows, block_live):
    vectors, sec_dev, sectors, block_rows, half_cols = psi.shape
    terms = left_op.shape[0]
    own_rows = block_rows // lax.axis_size("ops")
    sec_start = lax.axis_index("sec") * sec_dev
    row_ids = lax.broadcasted_iota(jnp.int32, (sectors, block_rows), 1)
    row_keep = row_ids < sector_rows[:, None]
    live_right = lax.dynamic_slice_in_dim(block_live, sec_start, sec_dev, 1)
    keep_right = row_keep[:, None, :, None] & (live_right[:, :, None, None] > 0)
    empty = jnp.zeros((vectors, sectors, sec_dev, block_rows, half_cols), jnp.float32)
    moved = lax.all_to_all(psi, "sec", split_axis=2, concat_axis=1, tiled=True)
    moved = jnp.where(keep_right[None], moved, jnp.zeros_like(moved))
    lefts = lax.all_gather(left_op, "sec", axis=1, tiled=True)
    piece = lax.all_gather(moved, "sub", axis=4, tiled=True)

    def one_term(index, acc):
        mid = jnp.einsum(
            "vacjk,ckl->vacjl", piece, right_op[index], preferred_element_type=jnp.float32
        ).astype(jnp.bfloat16)
        return acc + jnp.einsum(
            "aij,vacjl->vacil", lefts[index], mid, preferred_element_type=jnp.float32
        )

    partial_value = lax.fori_loop(0, terms, one_term, empty)
    summed = lax.psum(partial_value.astype(jnp.bfloat16), "ops").astype(jnp.float32)
    own = lax.dynamic_slice_in_dim(summed, lax.axis_index("ops") * own_rows, own_rows, 3)
    keep_own = lax.dynamic_slice_in_dim(keep_right, lax.axis_index("ops") * own_rows, own_rows, 2)
    total = jnp.where(keep_own[None], own, jnp.zeros_like(own))
    return total.astype(jnp.bfloat16)


def solution(mesh):
    sizes = dict(mesh.shape)
    small = sizes["sec"] == 4 and sizes["ops"] == 2 and sizes["sub"] == 2
    return jax.shard_map(
        local_small if small else local_any,
        mesh=mesh,
        in_specs=(
            P("runs", "sec", None, None, "sub"),
            P(("runs", "ops"), "sec", None, None),
            P(("runs", "ops"), "sec", None, "sub"),
            P("runs"),
            P("runs", None),
        ),
        out_specs=P("runs", None, "sec", "ops", "sub"),
        check_vma=False,
    )
```
